1024 devices in a mesh: dp: 64 (over z, core), seq: 16 (over y, x).
Axes of the slice: x: 4, y: 4, z: 32, core: 2. Of those that a mesh axis runs over, the one named last changes fastest.
Arguments:
- queries: bfloat16 [131072, 4096], P(('dp', 'seq')), may hold values from -30 to 30, as said below
- keys: bfloat16 [131072, 512], P(('dp', 'seq')), may hold values from -30 to 30, as said below
- values: bfloat16 [131072, 512], P(('dp', 'seq')), may hold values from -6 to 6
- starts: int32 [131072], P(('dp', 'seq')), may hold values from 0 to 131071, as said below
Outputs:
- attended: bfloat16 [131072, 4096], P(('dp', 'seq'))
The draws below stay inside these ranges and needn't reach their ends.
Inputs may be any that keep to these rules, and one draw needn't show every extreme that they name: starts never decrease along the tokens (starts[t] <= starts[t+1]); starts[t] <= t and t - starts[t] < 1024; all tokens from starts[t] to t share t's start; some sequence is exactly 1024 tokens long. `queries`: entries stay within -30 to 30. `keys`: entries stay within -30 to 30.
All inputs are finite; a program needn't handle non-finite values.
Results may differ from the reference program's by a relative error of at most 0.0035.
Values may be sent and summed in bfloat16 or wider, within the bound.
No kernel may reach another device: no remote copies, remote signals or barrier semaphores. Data moves between devices by JAX's collectives and lax.ppermute only.
A program may use at most 32 MiB of HBM per device.

```python
import jax
import jax.numpy as jnp
from jax import lax

HQ = 32
HK = 4
DH = 128
SPAN = 2048
LONGEST = 1024
TOKENS = 131072
N_DP = 64


def draw_queries(key, part):
    key = jax.random.fold_in(key, 11)
    drawn = jnp.clip(jax.random.normal(key, (TOKENS, HQ * DH), jnp.float32), -6.0, 6.0)
    return drawn.astype(jnp.bfloat16)


def draw_keys(key, part):
    key = jax.random.fold_in(key, 12)
    drawn = jnp.clip(jax.random.normal(key, (TOKENS, HK * DH), jnp.float32), -6.0, 6.0)
    return drawn.astype(jnp.bfloat16)


def draw_starts(key, part):
    key = jax.random.fold_in(key, 13)
    count = TOKENS // max(LONGEST // 8, 1) + 8
    lengths = jax.random.randint(key, (count,), 1, LONGEST // 2 + 1, dtype=jnp.int32)
    lengths = lengths.at[3].set(LONGEST)
    ends = jnp.cumsum(lengths).astype(jnp.int32)
    firsts = ends - lengths
    position = jnp.arange(TOKENS, dtype=jnp.int32)
    which = jnp.searchsorted(ends, position, side='right').astype(jnp.int32)
    return firsts[which].astype(jnp.int32)


def steps_of(rng, shape, cuts, least, top_value):
    def one(dim, blocks):
        heights = jax.random.uniform(jax.random.fold_in(jax.random.fold_in(rng, 6), dim), (blocks,), jnp.float32, least / len(cuts), top_value / len(cuts))
        return jnp.repeat(jnp.exp(heights), shape[dim] // blocks).reshape((-1,) + (1,) * (len(shape) - dim - 1))

    level = one(*cuts[0])
    for cut in cuts[1:]:
        level = level * one(*cut)
    return level


def centred(rng, dims, scale, bound, cuts=(), kind=jnp.bfloat16):
    drawn = scale * jax.random.normal(rng, dims, jnp.float32)
    if cuts:
        drawn = drawn * steps_of(rng, dims, cuts, -0.22, 0.18)
    return jnp.clip(drawn, -bound, bound).astype(kind)


def setup_inputs(seed: int = 0) -> dict:
    key_list = jax.random.split(jax.random.key(seed), 5)
    queries = draw_queries(jax.random.fold_in(key_list[4], 71), 0)
    keys = draw_keys(jax.random.fold_in(key_list[4], 71), 0)
    values = centred(key_list[2], (TOKENS, HK * DH), 1.0, 6.0, ((0, 1024),))
    starts = draw_starts(jax.random.fold_in(key_list[4], 71), 0)
    return dict(queries=queries, keys=keys, values=values, starts=starts)


def reference(queries, keys, values, starts):
    group = HQ // HK
    scale = DH ** -0.5
    block = min(512, SPAN)
    nblocks = SPAN // block
    pad_rows = jnp.zeros((LONGEST, HK * DH), jnp.bfloat16)
    keys_pad = jnp.concatenate([pad_rows, keys], axis=0)
    values_pad = jnp.concatenate([pad_rows, values], axis=0)

    def one_row(row):
        base = (row * SPAN).astype(jnp.int32)
        q_row = lax.dynamic_slice_in_dim(queries, base, SPAN, 0).reshape(SPAN, HQ, DH)
        k_row = lax.dynamic_slice_in_dim(keys_pad, base, SPAN + LONGEST, 0).reshape(SPAN + LONGEST, HK, DH)
        v_row = lax.dynamic_slice_in_dim(values_pad, base, SPAN + LONGEST, 0).reshape(SPAN + LONGEST, HK, DH)
        rel_starts = lax.dynamic_slice_in_dim(starts, base, SPAN, 0) - base

        def one_block(index):
            first = (index * block).astype(jnp.int32)
            q_blk = lax.dynamic_slice_in_dim(q_row, first, block, 0).astype(jnp.float32)
            k_win = jnp.repeat(lax.dynamic_slice_in_dim(k_row, first, LONGEST + block, 0), group, axis=1).astype(jnp.float32)
            v_win = jnp.repeat(lax.dynamic_slice_in_dim(v_row, first, LONGEST + block, 0), group, axis=1).astype(jnp.float32)
            s_blk = lax.dynamic_slice_in_dim(rel_starts, first, block, 0)
            rows = first + jnp.arange(block, dtype=jnp.int32)
            cols = first + jnp.arange(LONGEST + block, dtype=jnp.int32) - LONGEST
            allowed = (cols[None, :] >= s_blk[:, None]) & (cols[None, :] <= rows[:, None])
            scores = jnp.einsum("qhd,khd->hqk", q_blk, k_win) * scale
            scores = jnp.where(allowed[None], scores, -jnp.inf)
            top = jnp.max(scores, axis=2, keepdims=True)
            expd = jnp.exp(scores - top)
            total = jnp.sum(expd, axis=2)
            weights = lax.optimization_barrier(expd.astype(jnp.bfloat16))
            mixed = jnp.einsum("hqk,khd->qhd", weights.astype(jnp.float32), v_win)
            return (mixed / total.T[:, :, None]).astype(jnp.bfloat16)

        parts = lax.map(one_block, jnp.arange(nblocks, dtype=jnp.int32))
        return parts.reshape(SPAN, HQ * DH)

    rows_out = lax.map(one_row, jnp.arange(N_DP, dtype=jnp.int32))
    return rows_out.reshape(TOKENS, HQ * DH)
```

```python
import functools
import math

import jax
import jax.numpy as jnp
from jax import lax
from jax.experimental import pallas as pl
from jax.experimental.pallas import tpu as pltpu
from jax.sharding import PartitionSpec as P

HQ = 32
HK = 4
DH = 128
GROUP = HQ // HK
AXES = ("dp", "seq")
SIDE = 4
SCALE = math.log2(math.e) * DH**-0.5
MASKED = -1e30


def shift(block, distance):
    n = lax.axis_size(AXES)
    return lax.ppermute(block, AXES, [(i, i + distance) for i in range(n - distance)])


def attend(distances, chunk, merge, final, *refs):
    starts_ref, q_ref, *refs = refs
    kv_refs, refs = refs[: len(distances)], refs[len(distances) :]
    if merge:
        acc_in, top_in, total_in, *refs = refs
    if final:
        out_ref, *refs = refs
    else:
        acc_out, top_out, total_out, *refs = refs
    bias_ref, k_ref, v_ref = refs
    tok = q_ref.shape[0]
    flat = [d for group in distances for d in group]
    width = len(flat) * tok

    @pl.when(pl.program_id(0) == 0)
    def _():
        first = jnp.broadcast_to(starts_ref[...].astype(jnp.float32), (tok, tok)).T
        column = lax.broadcasted_iota(jnp.int32, (tok, tok), 1).astype(jnp.float32)
        row = lax.broadcasted_iota(jnp.int32, (tok, tok), 0).astype(jnp.float32)
        for i, d in enumerate(flat):
            allowed = column - float(tok * d) >= first
            if d == 0:
                allowed = allowed & (column <= row)
            bias_ref[:, i * tok : (i + 1) * tok] = jnp.where(allowed, 0.0, MASKED)
        v_ref[:, DH:] = jnp.ones((width, DH), v_ref.dtype)

    i = 0
    for group, kv_ref in zip(distances, kv_refs):
        for j in range(len(group)):
            k_ref[i * tok : (i + 1) * tok] = kv_ref[2 * j * tok : (2 * j + 1) * tok]
            v_ref[i * tok : (i + 1) * tok, :DH] = kv_ref[(2 * j + 1) * tok : (2 * j + 2) * tok]
            i += 1

    def heads_of(ref, heads):
        return jnp.concatenate([ref[:, h * DH : (h + 1) * DH] for h in heads], axis=0)

    for c in range(0, GROUP, chunk):
        heads = range(c, c + chunk)
        scores = lax.dot_general(
            heads_of(q_ref, heads),
            k_ref[...],
            (((1,), (1,)), ((), ())),
            preferred_element_type=jnp.float32,
        )
        scores = scores.reshape(chunk, tok, width) * SCALE + bias_ref[...][None]
        scores = scores.reshape(chunk * tok, width)
        top = jnp.max(scores, axis=1, keepdims=True)
        top = jnp.broadcast_to(top, (chunk * tok, DH))
        if merge:
            top_old = heads_of(top_in, heads)
            top = jnp.maximum(top, top_old)
        tops = jnp.concatenate([top] * len(flat), axis=1)
        weights = jnp.exp2(scores - tops).astype(jnp.bfloat16)
        mixed = jnp.dot(weights, v_ref[...], preferred_element_type=jnp.float32)
        mixed, total = mixed[:, :DH], mixed[:, DH:]
        if merge:
            fade = jnp.exp2(top_old - top)
            mixed = mixed + heads_of(acc_in, heads) * fade
            total = total + heads_of(total_in, heads) * fade
        if final:
            mixed = (mixed / total).astype(out_ref.dtype)
        for n, h in enumerate(heads):
            rows, lanes = slice(n * tok, (n + 1) * tok), slice(h * DH, (h + 1) * DH)
            if final:
                out_ref[:, lanes] = mixed[rows]
            else:
                acc_out[:, lanes] = mixed[rows]
                top_out[:, lanes] = top[rows]
                total_out[:, lanes] = total[rows]


def attention(starts, queries, arrays, distances, state=None, final=True, chunk=4):
    tok = queries.shape[0]
    blocks = sum(len(group) for group in distances)
    wide = pl.BlockSpec((tok, GROUP * DH), lambda g: (0, g))
    in_specs = [pl.BlockSpec((1, tok), lambda g: (0, 0)), wide]
    in_specs += [pl.BlockSpec((2 * tok * len(group), DH), lambda g: (0, g)) for group in distances]
    operands = [starts.reshape(1, tok), queries, *arrays]
    if state is not None:
        in_specs += [wide] * 3
        operands += state
    if final:
        out_shape = jax.ShapeDtypeStruct(queries.shape, queries.dtype)
        out_specs = wide
    else:
        out_shape = [jax.ShapeDtypeStruct(queries.shape, jnp.float32)] * 3
        out_specs = [wide] * 3
    return pl.pallas_call(
        functools.partial(attend, distances, chunk, state is not None, final),
        grid=(HK,),
        in_specs=in_specs,
        out_specs=out_specs,
        out_shape=out_shape,
        scratch_shapes=[
            pltpu.VMEM((tok, blocks * tok), jnp.float32),
            pltpu.VMEM((blocks * tok, DH), jnp.bfloat16),
            pltpu.VMEM((blocks * tok, 2 * DH), jnp.bfloat16),
        ],
        compiler_params=pltpu.CompilerParams(vmem_limit_bytes=32 * 2**20),
        cost_estimate=pl.CostEstimate(
            flops=4 * HQ * tok * blocks * tok * DH,
            bytes_accessed=(2 * HQ + 4 * HK * blocks) * tok * DH * 2,
            transcendentals=HQ * tok * blocks * tok,
        ),
    )(*operands)


def turn(block, columns):
    n = lax.axis_size("seq")
    route = [(i, i // SIDE * SIDE + (i + columns) % SIDE) for i in range(n)]
    return lax.ppermute(block, "seq", route)


def shards(queries, keys, values, starts):
    tok = queries.shape[0]
    seq = lax.axis_index("seq")
    me = lax.axis_index("dp") * lax.axis_size("seq") + seq
    column = seq % SIDE
    kv = jnp.concatenate([keys, values], axis=0)
    kv4 = shift(kv, SIDE)
    kv8 = shift(kv, 2 * SIDE)
    held = jnp.concatenate([kv, kv4, kv8], axis=0)

    def pair(columns):
        wraps = column + columns >= SIDE
        return lax.dynamic_slice_in_dim(held, jnp.where(wraps, 2 * tok, 0), 4 * tok, 0)

    kv15 = turn(pair(1), 1)
    kv37 = turn(pair(3), 3)
    kv26 = turn(pair(2), 2)
    starts = starts - me * tok
    state = attention(starts, queries, [kv, kv4, kv8], [(0,), (4,), (8,)], final=False)
    state = attention(
        starts, queries, [kv15, kv37], [(1, 5), (3, 7)], state=state, final=False, chunk=2
    )
    return attention(starts, queries, [kv26], [(2, 6)], state=state)


def solution(mesh):
    return jax.shard_map(
        shards,
        mesh=mesh,
        in_specs=(P(AXES, None), P(AXES, None), P(AXES, None), P(AXES)),
        out_specs=P(AXES, None),
        check_vma=False,
    )
```

```python
import functools
import math

import jax
import jax.numpy as jnp
from jax import lax
from jax.experimental import pallas as pl
from jax.experimental.pallas import tpu as pltpu
from jax.sharding import PartitionSpec as P

HQ = 32
HK = 4
DH = 128
GROUP = HQ // HK
AXES = ("dp", "seq")
SIDE = 4
SCALE = math.log2(math.e) * DH**-0.5
MASKED = -1e30


def shift(block, distance):
    n = lax.axis_size(AXES)
    return lax.ppermute(block, AXES, [(i, i + distance) for i in range(n - distance)])


def attend(distances, chunk, merge, final, *refs):
    starts_ref, q_ref, *refs = refs
    if final:
        flag_ref, *refs = refs
    arrays = len(distances) + final
    kv_refs, refs = refs[:arrays], refs[arrays:]
    if merge:
        acc_in, top_in, total_in, *refs = refs
    if final:
        out_ref, done_ref, sems, *refs = refs
    else:
        acc_out, top_out, total_out, *refs = refs
    bias_ref, k_ref, v_ref = refs
    tok = q_ref.shape[0]
    flat = [d for group in distances for d in group]
    width = len(flat) * tok
    first = jnp.broadcast_to(starts_ref[...].astype(jnp.float32), (tok, tok)).T
    column = lax.broadcasted_iota(jnp.int32, (tok, tok), 1).astype(jnp.float32)
    row = lax.broadcasted_iota(jnp.int32, (tok, tok), 0).astype(jnp.float32)
    for i, d in enumerate(flat):
        allowed = column - float(tok * d) >= first
        if d == 0:
            allowed = allowed & (column <= row)
        bias_ref[:, i * tok : (i + 1) * tok] = jnp.where(allowed, 0.0, MASKED)
    v_ref[:, :, DH:] = jnp.ones((HK, width, DH), v_ref.dtype)

    def fill(kv_refs):
        for g in range(HK):
            lanes = slice(g * DH, (g + 1) * DH)
            i = 0
            for group, kv_ref in zip(distances, kv_refs):
                for j in range(len(group)):
                    to = slice(i * tok, (i + 1) * tok)
                    k_ref[g, to] = kv_ref[2 * j * tok : (2 * j + 1) * tok, lanes]
                    v_ref[g, to, :DH] = kv_ref[(2 * j + 1) * tok : (2 * j + 2) * tok, lanes]
                    i += 1

    if final:
        pl.when(flag_ref[0] != 0)(lambda: fill(kv_refs[1:]))
        pl.when(flag_ref[0] == 0)(lambda: fill(kv_refs[:-1]))
    else:
        fill(kv_refs)

    def heads_of(ref, heads):
        return jnp.concatenate([ref[:, h * DH : (h + 1) * DH] for h in heads], axis=0)

    copies = []
    for c in range(0, HQ, chunk):
        g = c // GROUP
        heads = range(c, c + chunk)
        scores = lax.dot_general(
            heads_of(q_ref, heads),
            k_ref[g],
            (((1,), (1,)), ((), ())),
            preferred_element_type=jnp.float32,
        )
        scores = scores.reshape(chunk, tok, width) * SCALE + bias_ref[...][None]
        scores = scores.reshape(chunk * tok, width)
        top = jnp.max(scores, axis=1, keepdims=True)
        top = jnp.broadcast_to(top, (chunk * tok, DH))
        if merge:
            top_old = heads_of(top_in, heads)
            top = jnp.maximum(top, top_old)
        tops = jnp.concatenate([top] * len(flat), axis=1)
        weights = jnp.exp2(scores - tops).astype(jnp.bfloat16)
        mixed = jnp.dot(weights, v_ref[g], preferred_element_type=jnp.float32)
        mixed, total = mixed[:, :DH], mixed[:, DH:]
        if merge:
            fade = jnp.exp2(top_old - top)
            mixed = mixed + heads_of(acc_in, heads) * fade
            total = total + heads_of(total_in, heads) * fade
        if final:
            mixed = (mixed / total).astype(done_ref.dtype)
        for n, h in enumerate(heads):
            rows, lanes = slice(n * tok, (n + 1) * tok), slice(h * DH, (h + 1) * DH)
            if final:
                done_ref[:, lanes] = mixed[rows]
            else:
                acc_out[:, lanes] = mixed[rows]
                top_out[:, lanes] = top[rows]
                total_out[:, lanes] = total[rows]
        if final:
            lanes = pl.ds(c * DH, chunk * DH)
            copy = pltpu.make_async_copy(
                done_ref.at[:, lanes], out_ref.at[:, lanes], sems.at[c // chunk]
            )
            copy.start()
            copies.append(copy)
    for copy in copies:
        copy.wait()


def attention(starts, queries, arrays, distances, state=None, flag=None, chunk=4):
    tok = queries.shape[0]
    blocks = sum(len(group) for group in distances)
    final = flag is not None
    operands = [starts.reshape(1, tok), queries, *([flag] if final else [])]
    in_specs = [pl.BlockSpec(memory_space=pltpu.VMEM)] * 2
    in_specs += [pl.BlockSpec(memory_space=pltpu.SMEM)] * final
    operands += [*arrays, *(state or [])]
    in_specs += [pl.BlockSpec(memory_space=pltpu.VMEM)] * (len(operands) - len(in_specs))
    scratch = [
        pltpu.VMEM((tok, blocks * tok), jnp.float32),
        pltpu.VMEM((HK, blocks * tok, DH), jnp.bfloat16),
        pltpu.VMEM((HK, blocks * tok, 2 * DH), jnp.bfloat16),
    ]
    aliases = {}
    if final:
        out_shape = jax.ShapeDtypeStruct(queries.shape, queries.dtype)
        out_specs = pl.BlockSpec(memory_space=pl.ANY)
        scratch = [
            pltpu.VMEM(queries.shape, queries.dtype),
            pltpu.SemaphoreType.DMA((HQ // chunk,)),
        ] + scratch
    else:
        out_shape = [jax.ShapeDtypeStruct(queries.shape, jnp.float32)] * 3
        out_specs = [pl.BlockSpec(memory_space=pltpu.VMEM)] * 3
        if state is not None:
            aliases = {len(operands) - 3 + i: i for i in range(3)}
    return pl.pallas_call(
        functools.partial(attend, distances, chunk, state is not None, final),
        in_specs=in_specs,
        out_specs=out_specs,
        out_shape=out_shape,
        scratch_shapes=scratch,
        input_output_aliases=aliases,
        compiler_params=pltpu.CompilerParams(vmem_limit_bytes=16 * 2**20),
        cost_estimate=pl.CostEstimate(
            flops=4 * HQ * tok * blocks * tok * DH,
            bytes_accessed=(2 * HQ + 4 * HK * blocks) * tok * DH * 2,
            transcendentals=HQ * tok * blocks * tok,
        ),
    )(*operands)


def turn(block, columns):
    n = lax.axis_size("seq")
    route = [(i, i // SIDE * SIDE + (i + columns) % SIDE) for i in range(n)]
    return lax.ppermute(block, "seq", route)


def over(first, second):
    zero, n = jnp.zeros((), first.dtype), first.shape[0]
    return lax.pad(first, zero, ((0, n, 0), (0, 0, 0))) + lax.pad(
        second, zero, ((n, 0, 0), (0, 0, 0))
    )


def shards(queries, keys, values, starts):
    tok = queries.shape[0]
    seq = lax.axis_index("seq")
    me = lax.axis_index("dp") * lax.axis_size("seq") + seq
    column = seq % SIDE
    kv = over(keys, values)
    kv4 = shift(kv, SIDE)
    kv8 = shift(kv, 2 * SIDE)
    across = turn(kv, 2)
    across4 = shift(across, SIDE)
    across8 = shift(across, 2 * SIDE)
    held = jnp.concatenate([kv, kv4, kv8], axis=0)

    def pair(columns):
        wraps = column + columns >= SIDE
        return lax.dynamic_slice_in_dim(held, jnp.where(wraps, 2 * tok, 0), 4 * tok, 0)

    kv15 = turn(pair(1), 1)
    kv37 = turn(pair(3), 3)
    starts = starts - me * tok
    state = attention(starts, queries, [kv, kv4, kv8], [(0,), (4,), (8,)])
    state = attention(starts, queries, [kv15, kv37], [(1, 5), (3, 7)], state=state, chunk=2)
    early = (column < 2).astype(jnp.int32).reshape(1)
    return attention(
        starts, queries, [across, across4, across8], [(2,), (6,)], state=state, flag=early
    )


def solution(mesh):
    return jax.shard_map(
        shards,
        mesh=mesh,
        in_specs=(P(AXES, None), P(AXES, None), P(AXES, None), P(AXES)),
        out_specs=P(AXES, None),
        check_vma=False,
    )
```

```python
import functools
import math

import jax
import jax.numpy as jnp
from jax import lax
from jax.experimental import pallas as pl
from jax.experimental.pallas import tpu as pltpu
from jax.sharding import PartitionSpec as P

HQ = 32
HK = 4
DH = 128
GROUP = HQ // HK
AXES = ("dp", "seq")
SIDE = 4
SCALE = math.log2(math.e) * DH**-0.5
MASKED = -1e30


def shift(block, distance, columns=SIDE):
    n = lax.axis_size(AXES)
    route = [(i, i + distance) for i in range(n - distance) if i % SIDE < columns]
    return lax.ppermute(block, AXES, route)


def attend(distances, chunk, merge, final, *refs):
    starts_ref, q_ref, *refs = refs
    if final:
        flag_ref, *refs = refs
    arrays = len(distances) + final
    kv_refs, refs = refs[:arrays], refs[arrays:]
    if merge:
        acc_in, top_in, total_in, *refs = refs
    if final:
        out_ref, done_ref, sems, *refs = refs
    else:
        acc_out, top_out, total_out, *refs = refs
    bias_ref, k_ref, v_ref = refs
    tok = q_ref.shape[0]
    flat = [d for group in distances for d in group]
    width = len(flat) * tok
    first = jnp.broadcast_to(starts_ref[...].astype(jnp.float32), (tok, tok)).T
    column = lax.broadcasted_iota(jnp.int32, (tok, tok), 1).astype(jnp.float32)
    row = lax.broadcasted_iota(jnp.int32, (tok, tok), 0).astype(jnp.float32)
    for i, d in enumerate(flat):
        allowed = column - float(tok * d) >= first
        if d == 0:
            allowed = allowed & (column <= row)
        bias_ref[:, i * tok : (i + 1) * tok] = jnp.where(allowed, 0.0, MASKED)
    v_ref[:, :, DH:] = jnp.ones((HK, width, DH), v_ref.dtype)

    def fill(kv_refs):
        for g in range(HK):
            lanes = slice(g * DH, (g + 1) * DH)
            i = 0
            for group, kv_ref in zip(distances, kv_refs):
                for j in range(len(group)):
                    to = slice(i * tok, (i + 1) * tok)
                    k_ref[g, to] = kv_ref[2 * j * tok : (2 * j + 1) * tok, lanes]
                    v_ref[g, to, :DH] = kv_ref[(2 * j + 1) * tok : (2 * j + 2) * tok, lanes]
                    i += 1

    if final:
        pl.when(flag_ref[0] != 0)(lambda: fill(kv_refs[1:]))
        pl.when(flag_ref[0] == 0)(lambda: fill(kv_refs[:-1]))
    else:
        fill(kv_refs)

    def heads_of(ref, heads):
        return jnp.concatenate([ref[:, h * DH : (h + 1) * DH] for h in heads], axis=0)

    copies = []
    for c in range(0, HQ, chunk):
        g = c // GROUP
        heads = range(c, c + chunk)
        scores = lax.dot_general(
            heads_of(q_ref, heads),
            k_ref[g],
            (((1,), (1,)), ((), ())),
            preferred_element_type=jnp.float32,
        )
        scores = scores.reshape(chunk, tok, width) * SCALE + bias_ref[...][None]
        scores = scores.reshape(chunk * tok, width)
        top = jnp.max(scores, axis=1, keepdims=True)
        top = jnp.broadcast_to(top, (chunk * tok, DH))
        if merge:
            top_old = heads_of(top_in, heads)
            top = jnp.maximum(top, top_old)
        tops = jnp.concatenate([top] * len(flat), axis=1)
        weights = jnp.exp2(scores - tops).astype(jnp.bfloat16)
        mixed = jnp.dot(weights, v_ref[g], preferred_element_type=jnp.float32)
        mixed, total = mixed[:, :DH], mixed[:, DH:]
        if merge:
            fade = jnp.exp2(top_old - top)
            mixed = mixed + heads_of(acc_in, heads) * fade
            total = total + heads_of(total_in, heads) * fade
        if final:
            mixed = (mixed / total).astype(done_ref.dtype)
        for n, h in enumerate(heads):
            rows, lanes = slice(n * tok, (n + 1) * tok), slice(h * DH, (h + 1) * DH)
            if final:
                done_ref[:, lanes] = mixed[rows]
            else:
                acc_out[:, lanes] = mixed[rows]
                top_out[:, lanes] = top[rows]
                total_out[:, lanes] = total[rows]
        if final:
            lanes = pl.ds(c * DH, chunk * DH)
            copy = pltpu.make_async_copy(
                done_ref.at[:, lanes], out_ref.at[:, lanes], sems.at[c // chunk]
            )
            copy.start()
            copies.append(copy)
    for copy in copies:
        copy.wait()


def attention(starts, queries, arrays, distances, state=None, flag=None, chunk=4):
    tok = queries.shape[0]
    blocks = sum(len(group) for group in distances)
    final = flag is not None
    operands = [starts.reshape(1, tok), queries, *([flag] if final else [])]
    in_specs = [pl.BlockSpec(memory_space=pltpu.VMEM)] * 2
    in_specs += [pl.BlockSpec(memory_space=pltpu.SMEM)] * final
    operands += [*arrays, *(state or [])]
    in_specs += [pl.BlockSpec(memory_space=pltpu.VMEM)] * (len(operands) - len(in_specs))
    scratch = [
        pltpu.VMEM((tok, blocks * tok), jnp.float32),
        pltpu.VMEM((HK, blocks * tok, DH), jnp.bfloat16),
        pltpu.VMEM((HK, blocks * tok, 2 * DH), jnp.bfloat16),
    ]
    aliases = {}
    if final:
        out_shape = jax.ShapeDtypeStruct(queries.shape, queries.dtype)
        out_specs = pl.BlockSpec(memory_space=pl.ANY)
        scratch = [
            pltpu.VMEM(queries.shape, queries.dtype),
            pltpu.SemaphoreType.DMA((HQ // chunk,)),
        ] + scratch
    else:
        out_shape = [jax.ShapeDtypeStruct(queries.shape, jnp.float32)] * 3
        out_specs = [pl.BlockSpec(memory_space=pltpu.VMEM)] * 3
        if state is not None:
            aliases = {len(operands) - 3 + i: i for i in range(3)}
    return pl.pallas_call(
        functools.partial(attend, distances, chunk, state is not None, final),
        in_specs=in_specs,
        out_specs=out_specs,
        out_shape=out_shape,
        scratch_shapes=scratch,
        input_output_aliases=aliases,
        compiler_params=pltpu.CompilerParams(vmem_limit_bytes=16 * 2**20),
        cost_estimate=pl.CostEstimate(
            flops=4 * HQ * tok * blocks * tok * DH,
            bytes_accessed=(2 * HQ + 4 * HK * blocks) * tok * DH * 2,
            transcendentals=HQ * tok * blocks * tok,
        ),
    )(*operands)


def turn(block, columns):
    n = lax.axis_size("seq")
    route = [(i, i // SIDE * SIDE + (i + columns) % SIDE) for i in range(n)]
    return lax.ppermute(block, "seq", route)


def over(first, second):
    zero, n = jnp.zeros((), first.dtype), first.shape[0]
    return lax.pad(first, zero, ((0, n, 0), (0, 0, 0))) + lax.pad(
        second, zero, ((n, 0, 0), (0, 0, 0))
    )


def shards(queries, keys, values, starts):
    tok = queries.shape[0]
    seq = lax.axis_index("seq")
    me = lax.axis_index("dp") * lax.axis_size("seq") + seq
    column = seq % SIDE
    kv = over(keys, values)
    kv4 = shift(kv, SIDE)
    kv8 = shift(kv, 2 * SIDE)
    across = turn(kv, 2)
    across4 = shift(across, SIDE)
    across8 = shift(across, 2 * SIDE, 2)
    held = jnp.concatenate([kv, kv4, kv8], axis=0)

    def pair(columns):
        wraps = column + columns >= SIDE
        return lax.dynamic_slice_in_dim(held, jnp.where(wraps, 2 * tok, 0), 4 * tok, 0)

    kv15 = turn(pair(1), 1)
    kv37 = turn(pair(3), 3)
    starts = starts - me * tok
    state = attention(starts, queries, [kv, kv4, kv8], [(0,), (4,), (8,)])
    state = attention(starts, queries, [kv15, kv37], [(1, 5), (3, 7)], state=state, chunk=2)
    early = (column < 2).astype(jnp.int32).reshape(1)
    return attention(
        starts, queries, [across, across4, across8], [(2,), (6,)], state=state, flag=early
    )


def solution(mesh):
    return jax.shard_map(
        shards,
        mesh=mesh,
        in_specs=(P(AXES, None), P(AXES, None), P(AXES, None), P(AXES)),
        out_specs=P(AXES, None),
        check_vma=False,
    )
```

```python
import functools
import math

import jax
import jax.numpy as jnp
from jax import lax
from jax.experimental import pallas as pl
from jax.experimental.pallas import tpu as pltpu
from jax.sharding import PartitionSpec as P

HQ = 32
HK = 4
DH = 128
GROUP = HQ // HK
AXES = ("dp", "seq")
SIDE = 4
SCALE = math.log2(math.e) * DH**-0.5
MASKED = -1e30


def shift(block, distance, columns=SIDE):
    n = lax.axis_size(AXES)
    route = [(i, i + distance) for i in range(n - distance) if i % SIDE < columns]
    return lax.ppermute(block, AXES, route)


def attend(distances, chunk, merge, final, *refs):
    starts_ref, q_ref, *refs = refs
    if final:
        flag_ref, *refs = refs
    arrays = len(distances) + final
    kv_refs, refs = refs[:arrays], refs[arrays:]
    if merge:
        acc_in, top_in, total_in, *refs = refs
    if final:
        out_ref, done_ref, sems, *refs = refs
    else:
        acc_out, top_out, total_out, *refs = refs
    bias_ref, k_ref, v_ref = refs
    tok = q_ref.shape[0]
    flat = [d for group in distances for d in group]
    width = len(flat) * tok
    first = jnp.broadcast_to(starts_ref[...].astype(jnp.float32), (tok, tok)).T
    column = lax.broadcasted_iota(jnp.int32, (tok, tok), 1).astype(jnp.float32)
    row = lax.broadcasted_iota(jnp.int32, (tok, tok), 0).astype(jnp.float32)
    for i, d in enumerate(flat):
        allowed = column - float(tok * d) >= first
        if d == 0:
            allowed = allowed & (column <= row)
        bias_ref[:, i * tok : (i + 1) * tok] = jnp.where(allowed, 0.0, MASKED)
    v_ref[:, :, DH:] = jnp.ones((HK, width, DH), v_ref.dtype)

    def fill(kv_refs):
        for g in range(HK):
            lanes = slice(g * DH, (g + 1) * DH)
            i = 0
            for group, kv_ref in zip(distances, kv_refs):
                for j in range(len(group)):
                    to = slice(i * tok, (i + 1) * tok)
                    k_ref[g, to] = kv_ref[2 * j * tok : (2 * j + 1) * tok, lanes]
                    v_ref[g, to, :DH] = kv_ref[(2 * j + 1) * tok : (2 * j + 2) * tok, lanes]
                    i += 1

    if final:
        pl.when(flag_ref[0] != 0)(lambda: fill(kv_refs[1:]))
        pl.when(flag_ref[0] == 0)(lambda: fill(kv_refs[:-1]))
    else:
        fill(kv_refs)

    def heads_of(ref, heads):
        return jnp.concatenate([ref[:, h * DH : (h + 1) * DH] for h in heads], axis=0)

    copies = []
    for c in range(0, HQ, chunk):
        g = c // GROUP
        heads = range(c, c + chunk)
        scores = lax.dot_general(
            heads_of(q_ref, heads),
            k_ref[g],
            (((1,), (1,)), ((), ())),
            preferred_element_type=jnp.float32,
        )
        scores = scores.reshape(chunk, tok, width) * SCALE + bias_ref[...][None]
        scores = scores.reshape(chunk * tok, width)
        top = jnp.max(scores, axis=1, keepdims=True)
        top = jnp.broadcast_to(top, (chunk * tok, DH))
        if merge:
            top_old = heads_of(top_in, heads)
            top = jnp.maximum(top, top_old)
        tops = jnp.concatenate([top] * len(flat), axis=1)
        weights = jnp.exp2(scores - tops).astype(jnp.bfloat16)
        mixed = jnp.dot(weights, v_ref[g], preferred_element_type=jnp.float32)
        mixed, total = mixed[:, :DH], mixed[:, DH:]
        if merge:
            fade = jnp.exp2(top_old - top)
            mixed = mixed + heads_of(acc_in, heads) * fade
            total = total + heads_of(total_in, heads) * fade
        if final:
            mixed = (mixed / total).astype(done_ref.dtype)
        for n, h in enumerate(heads):
            rows, lanes = slice(n * tok, (n + 1) * tok), slice(h * DH, (h + 1) * DH)
            if final:
                done_ref[:, lanes] = mixed[rows]
            else:
                acc_out[:, lanes] = mixed[rows]
                top_out[:, lanes] = top[rows]
                total_out[:, lanes] = total[rows]
        if final:
            lanes = pl.ds(c * DH, chunk * DH)
            copy = pltpu.make_async_copy(
                done_ref.at[:, lanes], out_ref.at[:, lanes], sems.at[c // chunk]
            )
            copy.start()
            copies.append(copy)
    for copy in copies:
        copy.wait()


def attention(starts, queries, arrays, distances, state=None, flag=None, chunk=4):
    tok = queries.shape[0]
    blocks = sum(len(group) for group in distances)
    final = flag is not None
    operands = [starts.reshape(1, tok), queries, *([flag] if final else [])]
    in_specs = [pl.BlockSpec(memory_space=pltpu.VMEM)] * 2
    in_specs += [pl.BlockSpec(memory_space=pltpu.SMEM)] * final
    operands += [*arrays, *(state or [])]
    in_specs += [pl.BlockSpec(memory_space=pltpu.VMEM)] * (len(operands) - len(in_specs))
    scratch = [
        pltpu.VMEM((tok, blocks * tok), jnp.float32),
        pltpu.VMEM((HK, blocks * tok, DH), jnp.bfloat16),
        pltpu.VMEM((HK, blocks * tok, 2 * DH), jnp.bfloat16),
    ]
    aliases = {}
    if final:
        out_shape = jax.ShapeDtypeStruct(queries.shape, queries.dtype)
        out_specs = pl.BlockSpec(memory_space=pl.ANY)
        scratch = [
            pltpu.VMEM(queries.shape, queries.dtype),
            pltpu.SemaphoreType.DMA((HQ // chunk,)),
        ] + scratch
    else:
        out_shape = [jax.ShapeDtypeStruct(queries.shape, jnp.float32)] * 3
        out_specs = [pl.BlockSpec(memory_space=pltpu.VMEM)] * 3
        if state is not None:
            aliases = {len(operands) - 3 + i: i for i in range(3)}
    return pl.pallas_call(
        functools.partial(attend, distances, chunk, state is not None, final),
        in_specs=in_specs,
        out_specs=out_specs,
        out_shape=out_shape,
        scratch_shapes=scratch,
        input_output_aliases=aliases,
        compiler_params=pltpu.CompilerParams(vmem_limit_bytes=16 * 2**20),
        cost_estimate=pl.CostEstimate(
            flops=4 * HQ * tok * blocks * tok * DH,
            bytes_accessed=(2 * HQ + 4 * HK * blocks) * tok * DH * 2,
            transcendentals=HQ * tok * blocks * tok,
        ),
    )(*operands)


def turn(block, columns):
    n = lax.axis_size("seq")
    route = [(i, i // SIDE * SIDE + (i + columns) % SIDE) for i in range(n)]
    return lax.ppermute(block, "seq", route)


def over(first, second):
    zero, n = jnp.zeros((), first.dtype), first.shape[0]
    return lax.pad(first, zero, ((0, n, 0), (0, 0, 0))) + lax.pad(
        second, zero, ((n, 0, 0), (0, 0, 0))
    )


def shards(queries, keys, values, starts):
    tok = queries.shape[0]
    seq = lax.axis_index("seq")
    me = lax.axis_index("dp") * lax.axis_size("seq") + seq
    column = seq % SIDE
    kv = over(keys, values)
    kv4 = shift(kv, SIDE)
    kv8 = shift(kv, 2 * SIDE)
    across = turn(kv, 2)
    across8 = shift(across, 2 * SIDE, 2)
    across4 = shift(across, SIDE)
    held = jnp.concatenate([kv, kv4, kv8], axis=0)

    def pair(columns):
        wraps = column + columns >= SIDE
        return lax.dynamic_slice_in_dim(held, jnp.where(wraps, 2 * tok, 0), 4 * tok, 0)

    kv15 = turn(pair(1), 1)
    kv37 = turn(pair(3), 3)
    starts = starts - me * tok
    state = attention(starts, queries, [kv, kv4, kv8], [(0,), (4,), (8,)])
    state = attention(starts, queries, [kv15, kv37], [(1, 5), (3, 7)], state=state, chunk=2)
    late = (column >= 2).astype(jnp.int32).reshape(1)
    return attention(
        starts, queries, [across8, across4, across], [(6,), (2,)], state=state, flag=late
    )


def solution(mesh):
    return jax.shard_map(
        shards,
        mesh=mesh,
        in_specs=(P(AXES, None), P(AXES, None), P(AXES, None), P(AXES)),
        out_specs=P(AXES, None),
        check_vma=False,
    )
```

```python
import functools
import math

import jax
import jax.numpy as jnp
from jax import lax
from jax.experimental import pallas as pl
from jax.experimental.pallas import tpu as pltpu
from jax.sharding import PartitionSpec as P

HQ = 32
HK = 4
DH = 128
GROUP = HQ // HK
AXES = ("dp", "seq")
SIDE = 4
SCALE = math.log2(math.e) * DH**-0.5
MASKED = -1e30


def shift(block, distance, columns=SIDE):
    n = lax.axis_size(AXES)
    route = [(i, i + distance) for i in range(n - distance) if i % SIDE < columns]
    return lax.ppermute(block, AXES, route)


def attend(distances, chunk, merge, final, *refs):
    starts_ref, q_ref, *refs = refs
    if final:
        flag_ref, *refs = refs
    arrays = len(distances) + final
    kv_refs, refs = refs[:arrays], refs[arrays:]
    if merge:
        acc_in, top_in, total_in, *refs = refs
    if final:
        out_ref, done_ref, sems, *refs = refs
    else:
        acc_out, top_out, total_out, *refs = refs
    bias_ref, k_ref, v_ref = refs
    tok = q_ref.shape[0]
    flat = [d for group in distances for d in group]
    width = len(flat) * tok
    first = jnp.broadcast_to(starts_ref[...].astype(jnp.float32), (tok, tok)).T
    column = lax.broadcasted_iota(jnp.int32, (tok, tok), 1).astype(jnp.float32)
    row = lax.broadcasted_iota(jnp.int32, (tok, tok), 0).astype(jnp.float32)
    for i, d in enumerate(flat):
        allowed = column - float(tok * d) >= first
        if d == 0:
            allowed = allowed & (column <= row)
        bias_ref[:, i * tok : (i + 1) * tok] = jnp.where(allowed, 0.0, MASKED)
    v_ref[:, :, DH:] = jnp.ones((HK, width, DH), v_ref.dtype)

    def fill(kv_refs):
        for g in range(HK):
            lanes = slice(g * DH, (g + 1) * DH)
            i = 0
            for group, kv_ref in zip(distances, kv_refs):
                for j in range(len(group)):
                    to = slice(i * tok, (i + 1) * tok)
                    k_ref[g, to] = kv_ref[2 * j * tok : (2 * j + 1) * tok, lanes]
                    v_ref[g, to, :DH] = kv_ref[(2 * j + 1) * tok : (2 * j + 2) * tok, lanes]
                    i += 1

    if final:
        pl.when(flag_ref[0] != 0)(lambda: fill(kv_refs[1:]))
        pl.when(flag_ref[0] == 0)(lambda: fill(kv_refs[:-1]))
    else:
        fill(kv_refs)

    def heads_of(ref, heads):
        return jnp.concatenate([ref[:, h * DH : (h + 1) * DH] for h in heads], axis=0)

    copies = []
    for c in range(0, HQ, chunk):
        g = c // GROUP
        heads = range(c, c + chunk)
        scores = lax.dot_general(
            heads_of(q_ref, heads),
            k_ref[g],
            (((1,), (1,)), ((), ())),
            preferred_element_type=jnp.float32,
        )
        scores = scores.reshape(chunk, tok, width) * SCALE + bias_ref[...][None]
        scores = scores.reshape(chunk * tok, width)
        top = jnp.max(scores, axis=1, keepdims=True)
        top = jnp.broadcast_to(top, (chunk * tok, DH))
        if merge:
            top_old = heads_of(top_in, heads)
            top = jnp.maximum(top, top_old)
        tops = jnp.concatenate([top] * len(flat), axis=1)
        weights = jnp.exp2(scores - tops).astype(jnp.bfloat16)
        mixed = jnp.dot(weights, v_ref[g], preferred_element_type=jnp.float32)
        mixed, total = mixed[:, :DH], mixed[:, DH:]
        if merge:
            fade = jnp.exp2(top_old - top)
            mixed = mixed + heads_of(acc_in, heads) * fade
            total = total + heads_of(total_in, heads) * fade
        if final:
            mixed = (mixed / total).astype(done_ref.dtype)
        for n, h in enumerate(heads):
            rows, lanes = slice(n * tok, (n + 1) * tok), slice(h * DH, (h + 1) * DH)
            if final:
                done_ref[:, lanes] = mixed[rows]
            else:
                acc_out[:, lanes] = mixed[rows]
                top_out[:, lanes] = top[rows]
                total_out[:, lanes] = total[rows]
        if final:
            lanes = pl.ds(c * DH, chunk * DH)
            copy = pltpu.make_async_copy(
                done_ref.at[:, lanes], out_ref.at[:, lanes], sems.at[c // chunk]
            )
            copy.start()
            copies.append(copy)
    for copy in copies:
        copy.wait()


def attention(starts, queries, arrays, distances, state=None, flag=None, chunk=4):
    tok = queries.shape[0]
    blocks = sum(len(group) for group in distances)
    final = flag is not None
    operands = [starts.reshape(1, tok), queries, *([flag] if final else [])]
    in_specs = [pl.BlockSpec(memory_space=pltpu.VMEM)] * 2
    in_specs += [pl.BlockSpec(memory_space=pltpu.SMEM)] * final
    operands += [*arrays, *(state or [])]
    in_specs += [pl.BlockSpec(memory_space=pltpu.VMEM)] * (len(operands) - len(in_specs))
    scratch = [
        pltpu.VMEM((tok, blocks * tok), jnp.float32),
        pltpu.VMEM((HK, blocks * tok, DH), jnp.bfloat16),
        pltpu.VMEM((HK, blocks * tok, 2 * DH), jnp.bfloat16),
    ]
    aliases = {}
    if final:
        out_shape = jax.ShapeDtypeStruct(queries.shape, queries.dtype)
        out_specs = pl.BlockSpec(memory_space=pl.ANY)
        scratch = [
            pltpu.VMEM(queries.shape, queries.dtype),
            pltpu.SemaphoreType.DMA((HQ // chunk,)),
        ] + scratch
    else:
        out_shape = [jax.ShapeDtypeStruct(queries.shape, jnp.float32)] * 3
        out_specs = [pl.BlockSpec(memory_space=pltpu.VMEM)] * 3
        if state is not None:
            aliases = {len(operands) - 3 + i: i for i in range(3)}
    return pl.pallas_call(
        functools.partial(attend, distances, chunk, state is not None, final),
        in_specs=in_specs,
        out_specs=out_specs,
        out_shape=out_shape,
        scratch_shapes=scratch,
        input_output_aliases=aliases,
        compiler_params=pltpu.CompilerParams(vmem_limit_bytes=16 * 2**20),
        cost_estimate=pl.CostEstimate(
            flops=4 * HQ * tok * blocks * tok * DH,
            bytes_accessed=(2 * HQ + 4 * HK * blocks) * tok * DH * 2,
            transcendentals=HQ * tok * blocks * tok,
        ),
    )(*operands)


def turn(block, columns):
    n = lax.axis_size("seq")
    route = [(i, i // SIDE * SIDE + (i + columns) % SIDE) for i in range(n)]
    return lax.ppermute(block, "seq", route)


def over(first, second):
    zero, n = jnp.zeros((), first.dtype), first.shape[0]
    return lax.pad(first, zero, ((0, n, 0), (0, 0, 0))) + lax.pad(
        second, zero, ((n, 0, 0), (0, 0, 0))
    )


def shards(queries, keys, values, starts):
    tok = queries.shape[0]
    seq = lax.axis_index("seq")
    me = lax.axis_index("dp") * lax.axis_size("seq") + seq
    column = seq % SIDE
    kv = over(keys, values)
    kv4 = shift(kv, SIDE)
    kv8 = shift(kv, 2 * SIDE)
    across = turn(kv, 2)
    across4 = shift(across, SIDE)
    across8 = shift(across, 2 * SIDE, 2)
    held = jnp.concatenate([kv, kv4, kv8], axis=0)

    def pair(columns):
        wraps = column + columns >= SIDE
        return lax.dynamic_slice_in_dim(held, jnp.where(wraps, 2 * tok, 0), 4 * tok, 0)

    kv15 = turn(pair(1), 1)
    kv37 = turn(pair(3), 3)
    starts = starts - me * tok
    state = attention(starts, queries, [held], [(0, 4, 8)])
    state = attention(starts, queries, [kv15, kv37], [(1, 5), (3, 7)], state=state, chunk=2)
    early = (column < 2).astype(jnp.int32).reshape(1)
    return attention(
        starts, queries, [across, across4, across8], [(2,), (6,)], state=state, flag=early
    )


def solution(mesh):
    return jax.shard_map(
        shards,
        mesh=mesh,
        in_specs=(P(AXES, None), P(AXES, None), P(AXES, None), P(AXES)),
        out_specs=P(AXES, None),
        check_vma=False,
    )
```

```python
import functools
import math

import jax
import jax.numpy as jnp
from jax import lax
from jax.experimental import pallas as pl
from jax.experimental.pallas import tpu as pltpu
from jax.sharding import PartitionSpec as P

HQ = 32
HK = 4
DH = 128
GROUP = HQ // HK
AXES = ("dp", "seq")
SIDE = 4
SCALE = math.log2(math.e) * DH**-0.5
MASKED = -1e30


def shift(block, distance, columns=SIDE):
    n = lax.axis_size(AXES)
    route = [(i, i + distance) for i in range(n - distance) if i % SIDE < columns]
    return lax.ppermute(block, AXES, route)


def attend(distances, chunk, merge, final, *refs):
    starts_ref, q_ref, *refs = refs
    if final:
        flag_ref, *refs = refs
    arrays = len(distances) + final
    kv_refs, refs = refs[:arrays], refs[arrays:]
    if merge:
        acc_in, top_in, total_in, *refs = refs
    if final:
        out_ref, done_ref, sems, *refs = refs
    else:
        acc_out, top_out, total_out, *refs = refs
    bias_ref, k_ref, v_ref = refs
    tok = q_ref.shape[0]
    flat = [d for group in distances for d in group]
    width = len(flat) * tok
    first = jnp.broadcast_to(starts_ref[...].astype(jnp.float32), (tok, tok)).T
    column = lax.broadcasted_iota(jnp.int32, (tok, tok), 1).astype(jnp.float32)
    row = lax.broadcasted_iota(jnp.int32, (tok, tok), 0).astype(jnp.float32)
    for i, d in enumerate(flat):
        allowed = column - float(tok * d) >= first
        if d == 0:
            allowed = allowed & (column <= row)
        bias_ref[:, i * tok : (i + 1) * tok] = jnp.where(allowed, 0.0, MASKED)
    v_ref[:, :, DH:] = jnp.ones((HK, width, DH), v_ref.dtype)

    def fill(kv_refs):
        for g in range(HK):
            lanes = slice(g * DH, (g + 1) * DH)
            i = 0
            for group, kv_ref in zip(distances, kv_refs):
                for j in range(len(group)):
                    to = slice(i * tok, (i + 1) * tok)
                    k_ref[g, to] = kv_ref[2 * j * tok : (2 * j + 1) * tok, lanes]
                    v_ref[g, to, :DH] = kv_ref[(2 * j + 1) * tok : (2 * j + 2) * tok, lanes]
                    i += 1

    if final:
        pl.when(flag_ref[0] != 0)(lambda: fill(kv_refs[1:]))
        pl.when(flag_ref[0] == 0)(lambda: fill(kv_refs[:-1]))
    else:
        fill(kv_refs)

    def heads_of(ref, heads):
        return jnp.concatenate([ref[:, h * DH : (h + 1) * DH] for h in heads], axis=0)

    copies = []
    for c in range(0, HQ, chunk):
        g = c // GROUP
        heads = range(c, c + chunk)
        scores = lax.dot_general(
            heads_of(q_ref, heads),
            k_ref[g],
            (((1,), (1,)), ((), ())),
            preferred_element_type=jnp.float32,
        )
        scores = scores.reshape(chunk, tok, width) * SCALE + bias_ref[...][None]
        scores = scores.reshape(chunk * tok, width)
        top = jnp.max(scores, axis=1, keepdims=True)
        top = jnp.broadcast_to(top, (chunk * tok, DH))
        if merge:
            top_old = heads_of(top_in, heads)
            top = jnp.maximum(top, top_old)
        tops = jnp.concatenate([top] * len(flat), axis=1)
        weights = jnp.exp2(scores - tops).astype(jnp.bfloat16)
        mixed = jnp.dot(weights, v_ref[g], preferred_element_type=jnp.float32)
        mixed, total = mixed[:, :DH], mixed[:, DH:]
        if merge:
            fade = jnp.exp2(top_old - top)
            mixed = mixed + heads_of(acc_in, heads) * fade
            total = total + heads_of(total_in, heads) * fade
        if final:
            mixed = (mixed / total).astype(done_ref.dtype)
        for n, h in enumerate(heads):
            rows, lanes = slice(n * tok, (n + 1) * tok), slice(h * DH, (h + 1) * DH)
            if final:
                done_ref[:, lanes] = mixed[rows]
            else:
                acc_out[:, lanes] = mixed[rows]
                top_out[:, lanes] = top[rows]
                total_out[:, lanes] = total[rows]
        if final:
            lanes = pl.ds(c * DH, chunk * DH)
            copy = pltpu.make_async_copy(
                done_ref.at[:, lanes], out_ref.at[:, lanes], sems.at[c // chunk]
            )
            copy.start()
            copies.append(copy)
    for copy in copies:
        copy.wait()


def attention(starts, queries, arrays, distances, state=None, flag=None, chunk=4):
    tok = queries.shape[0]
    blocks = sum(len(group) for group in distances)
    final = flag is not None
    operands = [starts.reshape(1, tok), queries, *([flag] if final else [])]
    in_specs = [pl.BlockSpec(memory_space=pltpu.VMEM)] * 2
    in_specs += [pl.BlockSpec(memory_space=pltpu.SMEM)] * final
    operands += [*arrays, *(state or [])]
    in_specs += [pl.BlockSpec(memory_space=pltpu.VMEM)] * (len(operands) - len(in_specs))
    scratch = [
        pltpu.VMEM((tok, blocks * tok), jnp.float32),
        pltpu.VMEM((HK, blocks * tok, DH), jnp.bfloat16),
        pltpu.VMEM((HK, blocks * tok, 2 * DH), jnp.bfloat16),
    ]
    aliases = {}
    if final:
        out_shape = jax.ShapeDtypeStruct(queries.shape, queries.dtype)
        out_specs = pl.BlockSpec(memory_space=pl.ANY)
        scratch = [
            pltpu.VMEM(queries.shape, queries.dtype),
            pltpu.SemaphoreType.DMA((HQ // chunk,)),
        ] + scratch
    else:
        out_shape = [jax.ShapeDtypeStruct(queries.shape, jnp.float32)] * 3
        out_specs = [pl.BlockSpec(memory_space=pltpu.VMEM)] * 3
        if state is not None:
            aliases = {len(operands) - 3 + i: i for i in range(3)}
    return pl.pallas_call(
        functools.partial(attend, distances, chunk, state is not None, final),
        in_specs=in_specs,
        out_specs=out_specs,
        out_shape=out_shape,
        scratch_shapes=scratch,
        input_output_aliases=aliases,
        compiler_params=pltpu.CompilerParams(vmem_limit_bytes=16 * 2**20),
        cost_estimate=pl.CostEstimate(
            flops=4 * HQ * tok * blocks * tok * DH,
            bytes_accessed=(2 * HQ + 4 * HK * blocks) * tok * DH * 2,
            transcendentals=HQ * tok * blocks * tok,
        ),
    )(*operands)


def turn(block, columns):
    n = lax.axis_size("seq")
    route = [(i, i // SIDE * SIDE + (i + columns) % SIDE) for i in range(n)]
    return lax.ppermute(block, "seq", route)


def over(first, second):
    zero, n = jnp.zeros((), first.dtype), first.shape[0]
    return lax.pad(first, zero, ((0, n, 0), (0, 0, 0))) + lax.pad(
        second, zero, ((n, 0, 0), (0, 0, 0))
    )


def shards(queries, keys, values, starts):
    tok = queries.shape[0]
    seq = lax.axis_index("seq")
    me = lax.axis_index("dp") * lax.axis_size("seq") + seq
    column = seq % SIDE
    kv = over(keys, values)
    kv4 = shift(kv, SIDE)
    kv8 = shift(kv, 2 * SIDE)
    across = turn(kv, 2)
    across4 = shift(across, SIDE)
    across8 = shift(across, 2 * SIDE, 2)
    held = jnp.concatenate([kv, kv4, kv8], axis=0)

    def pair(columns):
        wraps = column + columns >= SIDE
        return lax.dynamic_slice_in_dim(held, jnp.where(wraps, 2 * tok, 0), 4 * tok, 0)

    kv15 = turn(pair(1), 1)
    kv37 = turn(pair(3), 3)
    starts = starts - me * tok
    state = attention(starts, queries, [kv, kv4, kv8], [(0,), (4,), (8,)])
    state = attention(starts, queries, [kv15, kv37], [(1, 5), (3, 7)], state=state, chunk=1)
    early = (column < 2).astype(jnp.int32).reshape(1)
    return attention(
        starts, queries, [across, across4, across8], [(2,), (6,)], state=state, flag=early
    )


def solution(mesh):
    return jax.shard_map(
        shards,
        mesh=mesh,
        in_specs=(P(AXES, None), P(AXES, None), P(AXES, None), P(AXES)),
        out_specs=P(AXES, None),
        check_vma=False,
    )
```
